256 devices in a mesh: dp: 4 (over x), vocab: 64 (over z, y, core).
Axes of the slice: x: 4, y: 4, z: 8, core: 2. Of those that a mesh axis runs over, the one named last changes fastest.
Arguments:
- hidden: bfloat16 [2048, 3072], P(('dp', 'vocab')), parts along dimension 0, may hold values from -60 to 60
- weight: bfloat16 [3072, 65536], P(None, 'vocab'), may hold values from -0.32421875 to 0.32421875
- targets: int32 [2048], P('dp'), parts along dimension 0, may hold values from 0 to 65535
Outputs:
- loss: float32 [4], P('dp'), parts along dimension 0
- d_hidden: bfloat16 [2048, 3072], P(('dp', 'vocab')), parts along dimension 0
- d_weight: bfloat16 [12288, 65536], P('dp', 'vocab'), parts along dimension 0
The draws below stay inside these ranges and needn't reach their ends.
There are 4 independent parts, one for each index of `dp`. The reference program is written for one: setup_inputs(seed, part) draws one part's arguments, and reference() takes and returns one part's arrays. A program takes and returns all parts, laid end to end along the dimension named above; an argument that names none is the same for every part. Nothing has to cross between parts.
All inputs are finite; a program needn't handle non-finite values.
Results may differ from the reference program's by a relative error of at most 0.0035.
Values may be sent and summed in bfloat16 or wider, within the bound.
No kernel may reach another device: no remote copies, remote signals or barrier semaphores. Data moves between devices by JAX's collectives and lax.ppermute only.
A program may use at most 64 MiB of HBM per device.

```python
import jax
import jax.numpy as jnp
from jax import lax

D = 3072
TOKENS = 512
VOCAB = 65536


def draw_hidden(key, part):
    first = jax.random.fold_in(jax.random.fold_in(key, 17), 0)
    values = jax.random.normal(first, (TOKENS, D), jnp.float32)
    return jnp.clip(values, -60.0, 60.0).astype(jnp.bfloat16)


def touch_ends(result, own_key, low, top_value):
    place = [jax.random.randint(jax.random.fold_in(own_key, axis), (), 0, length) for axis, length in enumerate(result.shape)]
    main_axis = result.shape.index(max(result.shape))
    neighbour = place[:main_axis] + [(place[main_axis] + 1) % result.shape[main_axis]] + place[main_axis + 1:]
    return result.at[tuple(place)].set(low).at[tuple(neighbour)].set(top_value)


def levels(key, dims, shards, least, high):
    level = 1.0
    for axis_at, parts in shards:
        steps = jax.random.uniform(jax.random.fold_in(jax.random.fold_in(key, 6), axis_at), (parts,), jnp.float32, least / len(shards), high / len(shards))
        level = level * jnp.repeat(jnp.exp(steps), dims[axis_at] // parts).reshape((-1,) + (1,) * (len(dims) - 1 - axis_at))
    return level


def noise(rng, extent, width, most, shards=(), kind=jnp.bfloat16):
    drawn = width * jax.random.normal(rng, extent, jnp.float32)
    if shards:
        drawn = drawn * levels(rng, extent, shards, -0.22, 0.18)
    return jnp.clip(drawn, -most, most).astype(kind)


def setup_inputs(seed: int = 0, part: int = 0) -> dict:
    key_list = jax.random.split(jax.random.key(seed), 4)
    part_keys = jax.random.split(jax.random.fold_in(key_list[3], part), 4)
    hidden = draw_hidden(jax.random.fold_in(jax.random.fold_in(key_list[3], part), 71), part)
    weight = noise(key_list[1], (D, VOCAB), (3 / D ** 0.5), 0.32421875, ((1, 64),))
    targets = touch_ends(jax.random.randint(part_keys[2], (TOKENS,), 0, VOCAB), jax.random.fold_in(part_keys[2], 1), 0, VOCAB - 1).astype(jnp.int32)
    return dict(hidden=hidden, weight=weight, targets=targets)


def reference(hidden, weight, targets):
    logits = jnp.dot(hidden, weight, preferred_element_type=jnp.float32)
    top = jnp.max(logits, axis=1)
    expo = jnp.exp(logits - top[:, None])
    total = jnp.sum(expo, axis=1)
    columns = lax.broadcasted_iota(jnp.int32, logits.shape, 1)
    hits = columns == targets.astype(jnp.int32)[:, None]
    picked = jnp.sum(jnp.where(hits, logits, jnp.zeros_like(logits)), axis=1)
    loss = jnp.mean(top + jnp.log(total) - picked).reshape(1)
    grad_logits = (expo / total[:, None] - hits.astype(logits.dtype)).astype(jnp.bfloat16)
    d_hidden = lax.dot_general(grad_logits, weight, (((1,), (1,)), ((), ())), preferred_element_type=jnp.float32).astype(jnp.bfloat16)
    d_weight = lax.dot_general(hidden, grad_logits, (((0,), (0,)), ((), ())), preferred_element_type=jnp.float32).astype(jnp.bfloat16)
    return loss, d_hidden, d_weight
```

```python
import jax
import jax.numpy as jnp
from jax import lax
from jax.sharding import Mesh
from jax.sharding import PartitionSpec as P

VOCAB = ("z", "y", "core")
DP_VOCAB = ("dp", "z", "y", "core")
SWAP = [(0, 1), (1, 0)]


def to_each(value, axis):
    devices = lax.axis_size(axis)
    return lax.all_to_all(
        jnp.broadcast_to(value[None], (devices, *value.shape)), axis, 0, 0, tiled=True
    )


def swapped(value):
    return lax.ppermute(value, "core", SWAP)


def combined(stats):
    top = jnp.max(stats[:, 0], axis=0)
    total = jnp.sum(stats[:, 1] * jnp.exp(stats[:, 0] - top[None]), axis=0)
    picked = jnp.sum(stats[:, 2], axis=0)
    return jnp.stack([top, total, picked])


def body(hidden, weight, targets):
    rows, depth = hidden.shape
    width = weight.shape[1]
    zs, ys = lax.axis_size("z"), lax.axis_size("y")
    core = lax.axis_index("core")

    other_weight = swapped(weight)
    mine = to_each(to_each(hidden, "z"), "y").reshape(ys * zs * rows, depth)
    theirs = swapped(mine)

    wanted = lax.dynamic_index_in_dim(targets.reshape(zs, ys, 2, rows), core, 2, keepdims=False)
    wanted = jnp.swapaxes(wanted, 0, 1).reshape(-1)
    chip = (lax.axis_index("z") * ys + lax.axis_index("y")) * 2
    lanes = lax.broadcasted_iota(jnp.int32, (1, width), 1)

    def logits_of(columns, at):
        logits = jnp.dot(mine, columns, preferred_element_type=jnp.float32)
        return logits, (chip + at) * width + lanes == wanted[:, None]

    first, first_hits = logits_of(weight, core)
    second, second_hits = logits_of(other_weight, 1 - core)

    top = jnp.maximum(jnp.max(first, axis=1), jnp.max(second, axis=1))
    total = jnp.sum(jnp.exp(first - top[:, None]), axis=1) + jnp.sum(
        jnp.exp(second - top[:, None]), axis=1
    )
    picked = jnp.sum(jnp.where(first_hits, first, 0.0), axis=1) + jnp.sum(
        jnp.where(second_hits, second, 0.0), axis=1
    )
    stats = jnp.stack([top, total, picked])
    stats = combined(to_each(combined(to_each(stats, "y")), "z"))
    top, total, picked = stats[0], stats[1], stats[2]

    part = jnp.sum(top + jnp.log(total) - picked).reshape(1)
    loss = (part + swapped(part)) / (2 * ys * zs * rows)

    def grad(logits, hits):
        return (jnp.exp(logits - top[:, None]) / total[:, None] - hits.astype(jnp.float32)).astype(
            jnp.bfloat16
        )

    first_grad, second_grad = grad(first, first_hits), grad(second, second_hits)

    def back(grads, columns):
        return lax.dot_general(
            grads, columns, (((1,), (1,)), ((), ())), preferred_element_type=jnp.float32
        )

    partial = (back(first_grad, weight) + back(second_grad, other_weight)).astype(jnp.bfloat16)
    near = lax.all_to_all(partial.reshape(ys, zs, rows, depth), "y", 0, 0, tiled=True)
    near = jnp.sum(near.astype(jnp.float32), axis=0)
    far = lax.all_to_all(near, "z", 0, 0, tiled=True)
    d_hidden = jnp.sum(far, axis=0).astype(jnp.bfloat16)

    both = jnp.concatenate([mine, theirs], axis=0)
    grads = jnp.concatenate([first_grad, swapped(second_grad)], axis=0)
    d_weight = lax.dot_general(
        both, grads, (((0,), (0,)), ((), ())), preferred_element_type=jnp.float32
    ).astype(jnp.bfloat16)
    return (loss, d_hidden, d_weight)


def solution(mesh):
    torus = Mesh(mesh.devices.reshape(mesh.shape["dp"], 8, 4, 2), DP_VOCAB)
    return jax.shard_map(
        body,
        mesh=torus,
        in_specs=(P(DP_VOCAB, None), P(None, VOCAB), P("dp")),
        out_specs=(P("dp"), P(DP_VOCAB, None), P("dp", VOCAB)),
        check_vma=False,
    )
```

```python
import functools

import jax
import jax.numpy as jnp
from jax import lax
from jax.experimental import pallas as pl
from jax.experimental.pallas import tpu as pltpu
from jax.sharding import Mesh
from jax.sharding import PartitionSpec as P

VOCAB = ("z", "y", "core")
DP_VOCAB = ("dp", "z", "y", "core")
SWAP = [(0, 1), (1, 0)]
VMEM_LIMIT = 24 * 1024 * 1024


def swapped(value):
    return lax.ppermute(value, "core", SWAP)


def shifted(value, axis, by):
    n = lax.axis_size(axis)
    return lax.ppermute(value, axis, [(i, (i + by) % n) for i in range(n)])


def shifts(n):
    return sorted(range(1, n), key=lambda k: -min(k, n - k))


def from_each(value, axis):
    n = lax.axis_size(axis)
    found = {k: shifted(value, axis, k) for k in shifts(n)}
    return [value] + [found[k] for k in range(1, n)]


def summed_back(pieces, axis):
    n = lax.axis_size(axis)
    found = [shifted(pieces[k], axis, -k) for k in shifts(n)]
    total = pieces[0].astype(jnp.float32)
    for piece in found:
        total = total + piece.astype(jnp.float32)
    return total


def rolled(value, dim, start, step):
    n = value.shape[dim]
    if step < 0:
        value = jnp.flip(value, dim)
        start = n - 1 - start
    twice = jnp.concatenate([value, value], axis=dim)
    return lax.dynamic_slice_in_dim(twice, lax.rem(start + n, n), n, dim)


def logits_kernel(h_ref, first_ref, second_ref, out_ref, *, half):
    @pl.when(pl.program_id(0) < half)
    def _():
        out_ref[...] = jnp.dot(h_ref[...], first_ref[...], preferred_element_type=jnp.float32)

    @pl.when(pl.program_id(0) >= half)
    def _():
        out_ref[...] = jnp.dot(h_ref[...], second_ref[...], preferred_element_type=jnp.float32)


def logits_of(mine, first, second, tile=256):
    rows, depth = mine.shape
    width = first.shape[1]
    half = width // tile
    return pl.pallas_call(
        functools.partial(logits_kernel, half=half),
        grid=(2 * half,),
        in_specs=[
            pl.BlockSpec((rows, depth), lambda i: (0, 0)),
            pl.BlockSpec((depth, tile), lambda i: (0, jnp.minimum(i, half - 1))),
            pl.BlockSpec((depth, tile), lambda i: (0, jnp.maximum(i - half, 0))),
        ],
        out_specs=pl.BlockSpec((rows, tile), lambda i: (0, i)),
        out_shape=jax.ShapeDtypeStruct((rows, 2 * width), jnp.float32),
        compiler_params=pltpu.CompilerParams(vmem_limit_bytes=VMEM_LIMIT),
        cost_estimate=pl.CostEstimate(
            flops=4 * rows * depth * width,
            bytes_accessed=4 * depth * width + 8 * rows * width,
            transcendentals=0,
        ),
    )(mine, first, second)


def back_kernel(g_ref, first_ref, second_ref, out_ref):
    width = first_ref.shape[1]
    dims = (((1,), (1,)), ((), ()))
    total = lax.dot_general(
        g_ref[:, :width], first_ref[...], dims, preferred_element_type=jnp.float32
    )
    total = total + lax.dot_general(
        g_ref[:, width:], second_ref[...], dims, preferred_element_type=jnp.float32
    )
    out_ref[...] = total.astype(out_ref.dtype)


def back_of(grads, first, second, tile=512):
    rows = grads.shape[0]
    depth, width = first.shape
    return pl.pallas_call(
        back_kernel,
        grid=(depth // tile,),
        in_specs=[
            pl.BlockSpec((rows, 2 * width), lambda i: (0, 0)),
            pl.BlockSpec((tile, width), lambda i: (i, 0)),
            pl.BlockSpec((tile, width), lambda i: (i, 0)),
        ],
        out_specs=pl.BlockSpec((rows, tile), lambda i: (0, i)),
        out_shape=jax.ShapeDtypeStruct((rows, depth), jnp.bfloat16),
        compiler_params=pltpu.CompilerParams(vmem_limit_bytes=VMEM_LIMIT),
        cost_estimate=pl.CostEstimate(
            flops=4 * rows * depth * width,
            bytes_accessed=4 * depth * width + 2 * rows * depth,
            transcendentals=0,
        ),
    )(grads, first, second)


def body(hidden, weight, targets):
    rows, depth = hidden.shape
    width = weight.shape[1]
    zs, ys = lax.axis_size("z"), lax.axis_size("y")
    z, y, core = (lax.axis_index(name) for name in VOCAB)
    tokens = ys * zs * rows

    other_weight = swapped(weight)
    line = jnp.concatenate(from_each(hidden, "z"), axis=0)
    mine = jnp.concatenate(from_each(line, "y"), axis=0)
    theirs = swapped(mine)

    wanted = lax.dynamic_index_in_dim(targets.reshape(zs, ys, 2, rows), core, 2, keepdims=False)
    wanted = jnp.swapaxes(wanted, 0, 1)
    wanted = rolled(rolled(wanted, 0, y, -1), 1, z, -1).reshape(tokens)
    chip = (z * ys + y) * 2
    lanes = lax.broadcasted_iota(jnp.int32, (1, 2 * width), 1)
    columns = chip * width + jnp.where(
        lanes < width, lanes + core * width, lanes - width + (1 - core) * width
    )
    hits = columns == wanted[:, None]

    logits = logits_of(mine, weight, other_weight)
    top = jnp.max(logits, axis=1)
    total = jnp.sum(jnp.exp(logits - top[:, None]), axis=1)
    picked = jnp.sum(jnp.where(hits, logits, 0.0), axis=1)

    stats = jnp.stack([top, total, picked]).reshape(3, ys, zs, rows)
    stats = rolled(rolled(stats, 1, y, -1), 2, z, -1).reshape(3, tokens)
    stats = lax.all_to_all(
        jnp.broadcast_to(stats[None], (zs * ys, 3, tokens)), ("z", "y"), 0, 0, tiled=True
    )
    top = jnp.max(stats[:, 0], axis=0)
    total = jnp.sum(stats[:, 1] * jnp.exp(stats[:, 0] - top[None]), axis=0)
    picked = jnp.sum(stats[:, 2], axis=0)

    part = jnp.sum(top + jnp.log(total) - picked).reshape(1)
    loss = (part + swapped(part)) / (2 * tokens)

    both = jnp.stack([top, total]).reshape(2, ys, zs, rows)
    both = rolled(rolled(both, 1, y, -1), 2, z, -1).reshape(2, tokens)
    grads = (
        jnp.exp(logits - both[0][:, None]) / both[1][:, None] - hits.astype(jnp.float32)
    ).astype(jnp.bfloat16)

    partial = back_of(grads, weight, other_weight).reshape(ys, zs * rows, depth)
    near = summed_back([partial[k] for k in range(ys)], "y").reshape(zs, rows, depth)
    d_hidden = summed_back([near[k] for k in range(zs)], "z").astype(jnp.bfloat16)

    hiddens = jnp.concatenate([mine, theirs], axis=0)
    own = jnp.concatenate([grads[:, :width], swapped(grads[:, width:])], axis=0)
    d_weight = lax.dot_general(
        hiddens, own, (((0,), (0,)), ((), ())), preferred_element_type=jnp.float32
    ).astype(jnp.bfloat16)
    return (loss, d_hidden, d_weight)


def solution(mesh):
    torus = Mesh(mesh.devices.reshape(mesh.shape["dp"], 8, 4, 2), DP_VOCAB)
    return jax.shard_map(
        body,
        mesh=torus,
        in_specs=(P(DP_VOCAB, None), P(None, VOCAB), P("dp")),
        out_specs=(P("dp"), P(DP_VOCAB, None), P("dp", VOCAB)),
        check_vma=False,
    )
```

```python
import jax
import jax.numpy as jnp
from jax import lax
from jax.experimental import pallas as pl
from jax.experimental.pallas import tpu as pltpu
from jax.sharding import Mesh
from jax.sharding import PartitionSpec as P

NEAR = ("zl", "y")
CHIPS = ("zh", "zl", "y")
VOCAB = ("zh", "zl", "y", "core")
DP_VOCAB = ("dp", "zh", "zl", "y", "core")
SWAP = [(0, 1), (1, 0)]
VMEM_LIMIT = 24 * 1024 * 1024
TILES = 8


def to_each(value, axis):
    devices = lax.axis_size(axis)
    return lax.all_to_all(
        jnp.broadcast_to(value[None], (devices, *value.shape)), axis, 0, 0, tiled=True
    )


def swapped(value):
    return lax.ppermute(value, "core", SWAP)


def logits_kernel(h_any, first_ref, second_ref, out_ref, h_ref, held, h_sem, sems):
    half = TILES // 2
    tile = held.shape[2]

    def copy(k):
        ref = first_ref if k < half else second_ref
        return pltpu.make_async_copy(
            ref.at[:, pl.ds((k % half) * tile, tile)], held.at[k], sems.at[k]
        )

    h_copy = pltpu.make_async_copy(h_any, h_ref, h_sem)
    h_copy.start()
    for k in range(TILES):
        copy(k).start()
    h_copy.wait()
    for k in range(TILES):
        copy(k).wait()
        out_ref[:, pl.ds(k * tile, tile)] = jnp.dot(
            h_ref[...], held[k], preferred_element_type=jnp.float32
        )


def logits_of(mine, first, second):
    rows, depth = mine.shape
    width = first.shape[1]
    return pl.pallas_call(
        logits_kernel,
        in_specs=[pl.BlockSpec(memory_space=pl.ANY)] * 3,
        out_specs=pl.BlockSpec(memory_space=pltpu.VMEM),
        out_shape=jax.ShapeDtypeStruct((rows, 2 * width), jnp.float32),
        scratch_shapes=[
            pltpu.VMEM((rows, depth), jnp.bfloat16),
            pltpu.VMEM((TILES, depth, 2 * width // TILES), jnp.bfloat16),
            pltpu.SemaphoreType.DMA,
            pltpu.SemaphoreType.DMA((TILES,)),
        ],
        compiler_params=pltpu.CompilerParams(vmem_limit_bytes=VMEM_LIMIT),
        cost_estimate=pl.CostEstimate(
            flops=4 * rows * depth * width,
            bytes_accessed=4 * depth * width + 8 * rows * width,
            transcendentals=0,
        ),
    )(mine, first, second)


def back_kernel(g_ref, first_ref, second_ref, out_ref, first_held, second_held, sems):
    width = first_ref.shape[1]
    tile = first_held.shape[1]
    dims = (((1,), (1,)), ((), ()))

    def copies(k):
        rows = pl.ds(k * tile, tile)
        return (
            pltpu.make_async_copy(first_ref.at[rows], first_held.at[k], sems.at[0, k]),
            pltpu.make_async_copy(second_ref.at[rows], second_held.at[k], sems.at[1, k]),
        )

    for k in range(TILES):
        for copy in copies(k):
            copy.start()
    for k in range(TILES):
        for copy in copies(k):
            copy.wait()
        total = lax.dot_general(
            g_ref[:, :width], first_held[k], dims, preferred_element_type=jnp.float32
        ) + lax.dot_general(
            g_ref[:, width:], second_held[k], dims, preferred_element_type=jnp.float32
        )
        out_ref[:, pl.ds(k * tile, tile)] = total.astype(out_ref.dtype)


def back_of(grads, first, second):
    rows = grads.shape[0]
    depth, width = first.shape
    held = pltpu.VMEM((TILES, depth // TILES, width), jnp.bfloat16)
    return pl.pallas_call(
        back_kernel,
        in_specs=[
            pl.BlockSpec(memory_space=pltpu.VMEM),
            pl.BlockSpec(memory_space=pl.ANY),
            pl.BlockSpec(memory_space=pl.ANY),
        ],
        out_specs=pl.BlockSpec(memory_space=pltpu.VMEM),
        out_shape=jax.ShapeDtypeStruct((rows, depth), jnp.bfloat16),
        scratch_shapes=[held, held, pltpu.SemaphoreType.DMA((2, TILES))],
        compiler_params=pltpu.CompilerParams(vmem_limit_bytes=VMEM_LIMIT),
        cost_estimate=pl.CostEstimate(
            flops=4 * rows * depth * width,
            bytes_accessed=4 * depth * width + 2 * rows * depth,
            transcendentals=0,
        ),
    )(grads, first, second)


def body(hidden, weight, targets):
    rows, depth = hidden.shape
    width = weight.shape[1]
    far, near, ys = lax.axis_size("zh"), lax.axis_size(NEAR), lax.axis_size("y")
    core = lax.axis_index("core")
    tokens = far * near * rows

    weight = pltpu.with_memory_space_constraint(weight, pltpu.HBM)
    other_weight = pltpu.with_memory_space_constraint(swapped(weight), pltpu.HBM)
    mine = to_each(to_each(hidden, "zh"), NEAR).reshape(tokens, depth)
    theirs = swapped(mine)

    wanted = targets.reshape(far, near, 2, rows)
    wanted = lax.dynamic_index_in_dim(wanted, core, 2, keepdims=False)
    wanted = jnp.swapaxes(wanted, 0, 1).reshape(tokens)
    chip = lax.axis_index(CHIPS) * 2
    lanes = lax.broadcasted_iota(jnp.int32, (1, 2 * width), 1)
    columns = chip * width + jnp.where(
        lanes < width, lanes + core * width, lanes - width + (1 - core) * width
    )
    hits = columns == wanted[:, None]

    logits = logits_of(pltpu.with_memory_space_constraint(mine, pltpu.HBM), weight, other_weight)
    top = jnp.max(logits, axis=1)
    total = jnp.sum(jnp.exp(logits - top[:, None]), axis=1)
    picked = jnp.sum(jnp.where(hits, logits, 0.0), axis=1)
    stats = to_each(jnp.stack([top, total, picked]), CHIPS)
    top = jnp.max(stats[:, 0], axis=0)
    total = jnp.sum(stats[:, 1] * jnp.exp(stats[:, 0] - top[None]), axis=0)
    picked = jnp.sum(stats[:, 2], axis=0)

    part = jnp.sum(top + jnp.log(total) - picked).reshape(1)
    loss = (part + swapped(part)) / (2 * tokens)
    grads = (
        jnp.exp(logits - top[:, None]) / total[:, None] - hits.astype(jnp.float32)
    ).astype(jnp.bfloat16)

    partial = back_of(grads, weight, other_weight).reshape(near, far, rows, depth)
    summed = lax.all_to_all(partial, NEAR, 0, 0, tiled=True)
    summed = jnp.sum(summed.astype(jnp.float32), axis=0)
    summed = lax.all_to_all(summed, "zh", 0, 0, tiled=True)
    d_hidden = jnp.sum(summed, axis=0).astype(jnp.bfloat16)

    both = jnp.concatenate([mine, theirs], axis=0)
    own = jnp.concatenate([grads[:, :width], swapped(grads[:, width:])], axis=0)
    d_weight = lax.dot_general(
        both, own, (((0,), (0,)), ((), ())), preferred_element_type=jnp.float32
    ).astype(jnp.bfloat16)
    return (loss, d_hidden, d_weight)


def solution(mesh):
    torus = Mesh(mesh.devices.reshape(mesh.shape["dp"], 4, 2, 4, 2), DP_VOCAB)
    return jax.shard_map(
        body,
        mesh=torus,
        in_specs=(P(DP_VOCAB, None), P(None, VOCAB), P("dp")),
        out_specs=(P("dp"), P(DP_VOCAB, None), P("dp", VOCAB)),
        check_vma=False,
    )
```

```python
import jax
import jax.numpy as jnp
from jax import lax
from jax.experimental import pallas as pl
from jax.experimental.pallas import tpu as pltpu
from jax.sharding import Mesh
from jax.sharding import PartitionSpec as P

NEAR = ("zl", "y")
CHIPS = ("zh", "zl", "y")
VOCAB = ("zh", "zl", "y", "core")
DP_VOCAB = ("dp", "zh", "zl", "y", "core")
SWAP = [(0, 1), (1, 0)]
def to_each(value, axis):
    devices = lax.axis_size(axis)
    return lax.all_to_all(
        jnp.broadcast_to(value[None], (devices, *value.shape)), axis, 0, 0, tiled=True
    )


def swapped(value):
    return lax.ppermute(value, "core", SWAP)


def nothing_kernel(*refs):
    del refs


def after(value, first):
    return pl.pallas_call(
        nothing_kernel,
        in_specs=[pl.BlockSpec(memory_space=pl.ANY)] * 2,
        out_specs=pl.BlockSpec(memory_space=pl.ANY),
        out_shape=jax.ShapeDtypeStruct(value.shape, value.dtype),
        input_output_aliases={0: 0},
        compiler_params=pltpu.CompilerParams(vmem_limit_bytes=1024 * 1024),
        cost_estimate=pl.CostEstimate(flops=0, bytes_accessed=0, transcendentals=0),
    )(value, first)


def back(grads, columns):
    return lax.dot_general(
        grads, columns, (((1,), (1,)), ((), ())), preferred_element_type=jnp.float32
    )


def body(hidden, weight, targets):
    rows, depth = hidden.shape
    width = weight.shape[1]
    far, near, ys = lax.axis_size("zh"), lax.axis_size(NEAR), lax.axis_size("y")
    core = lax.axis_index("core")
    tokens = far * near * rows

    other_weight = swapped(weight)
    weights = [weight, other_weight]
    line = after(to_each(hidden, "zh"), other_weight[:16, :128])
    mine = to_each(line, NEAR).reshape(tokens, depth)
    theirs = swapped(mine)

    wanted = targets.reshape(far, near, 2, rows)
    wanted = lax.dynamic_index_in_dim(wanted, core, 2, keepdims=False)
    wanted = jnp.swapaxes(wanted, 0, 1).reshape(tokens)
    chip = lax.axis_index(CHIPS) * 2
    lanes = lax.broadcasted_iota(jnp.int32, (1, width), 1)
    hits = [(chip + at) * width + lanes == wanted[:, None] for at in (core, 1 - core)]
    target = sum(back(h.astype(jnp.bfloat16), w) for h, w in zip(hits, weights))
    target = lax.optimization_barrier(target.astype(jnp.bfloat16))

    logits = [jnp.dot(mine, w, preferred_element_type=jnp.float32) for w in weights]
    local_top = jnp.maximum(jnp.max(logits[0], axis=1), jnp.max(logits[1], axis=1))
    expo = [jnp.exp(x - local_top[:, None]) for x in logits]
    local_total = jnp.sum(expo[0], axis=1) + jnp.sum(expo[1], axis=1)
    local_picked = sum(jnp.sum(jnp.where(h, x, 0.0), axis=1) for h, x in zip(hits, logits))
    packed = jnp.stack([local_top, local_total, local_picked])
    stats = to_each(packed, CHIPS)

    local_top = after(packed, packed[1:2])[0]
    expo = [jnp.exp(x - local_top[:, None]) for x in logits]
    rest = [jnp.where(h, 0.0, e).astype(jnp.bfloat16) for h, e in zip(hits, expo)]
    others = lax.optimization_barrier(back(rest[0], weights[0]) + back(rest[1], weights[1]))

    top = jnp.max(stats[:, 0], axis=0)
    total = jnp.sum(stats[:, 1] * jnp.exp(stats[:, 0] - top[None]), axis=0)
    picked = jnp.sum(stats[:, 2], axis=0)
    factor = jnp.exp(local_top - top) / total
    at_target = (jnp.exp(picked - top) / total - 1.0).astype(jnp.bfloat16).astype(jnp.float32)
    partial = others * factor[:, None] + at_target[:, None] * target.astype(jnp.float32)
    partial = partial.astype(jnp.bfloat16).reshape(near, far, rows, depth)
    summed = lax.all_to_all(partial, NEAR, 0, 0, tiled=True)
    summed = jnp.sum(summed.astype(jnp.float32), axis=0)

    first_grad, second_grad = (
        (jnp.exp(x - top[:, None]) / total[:, None] - h.astype(jnp.float32)).astype(jnp.bfloat16)
        for x, h in zip(logits, hits)
    )
    both = jnp.concatenate([mine, theirs], axis=0)
    own = jnp.concatenate([first_grad, swapped(second_grad)], axis=0)
    d_weight = lax.dot_general(
        both, own, (((0,), (0,)), ((), ())), preferred_element_type=jnp.float32
    ).astype(jnp.bfloat16)

    summed = lax.all_to_all(after(summed, d_weight[:16, :128]), "zh", 0, 0, tiled=True)
    d_hidden = jnp.sum(summed, axis=0).astype(jnp.bfloat16)

    part = jnp.sum(top + jnp.log(total) - picked).reshape(1)
    loss = (part + swapped(part)) / (2 * tokens)
    return (loss, d_hidden, d_weight)


def solution(mesh):
    torus = Mesh(mesh.devices.reshape(mesh.shape["dp"], 4, 2, 4, 2), DP_VOCAB)
    return jax.shard_map(
        body,
        mesh=torus,
        in_specs=(P(DP_VOCAB, None), P(None, VOCAB), P("dp")),
        out_specs=(P("dp"), P(DP_VOCAB, None), P("dp", VOCAB)),
        check_vma=False,
    )
```

```python
import jax
import jax.numpy as jnp
from jax import lax
from jax.experimental import pallas as pl
from jax.experimental.pallas import tpu as pltpu
from jax.sharding import Mesh
from jax.sharding import PartitionSpec as P

NEAR = ("zl", "y")
CHIPS = ("zh", "zl", "y")
VOCAB = ("zh", "zl", "y", "core")
DP_VOCAB = ("dp", "zh", "zl", "y", "core")
SWAP = [(0, 1), (1, 0)]
def to_each(value, axis):
    devices = lax.axis_size(axis)
    return lax.all_to_all(
        jnp.broadcast_to(value[None], (devices, *value.shape)), axis, 0, 0, tiled=True
    )


def swapped(value):
    return lax.ppermute(value, "core", SWAP)


def nothing_kernel(*refs):
    del refs


def after(value, first):
    return pl.pallas_call(
        nothing_kernel,
        in_specs=[pl.BlockSpec(memory_space=pl.ANY)] * 2,
        out_specs=pl.BlockSpec(memory_space=pl.ANY),
        out_shape=jax.ShapeDtypeStruct(value.shape, value.dtype),
        input_output_aliases={0: 0},
        compiler_params=pltpu.CompilerParams(vmem_limit_bytes=1024 * 1024),
        cost_estimate=pl.CostEstimate(flops=0, bytes_accessed=0, transcendentals=0),
    )(value, first)


def back(grads, columns):
    return lax.dot_general(
        grads, columns, (((1,), (1,)), ((), ())), preferred_element_type=jnp.float32
    )


def body(hidden, weight, targets):
    rows, depth = hidden.shape
    width = weight.shape[1]
    far, near, ys = lax.axis_size("zh"), lax.axis_size(NEAR), lax.axis_size("y")
    core = lax.axis_index("core")
    tokens = far * near * rows

    other_weight = swapped(weight)
    weights = [weight, other_weight]
    line = after(to_each(hidden, "zh"), other_weight[:16, :128])
    mine = to_each(line, NEAR).reshape(tokens, depth)
    theirs = swapped(mine)

    wanted = targets.reshape(far, near, 2, rows)
    wanted = lax.dynamic_index_in_dim(wanted, core, 2, keepdims=False)
    wanted = jnp.swapaxes(wanted, 0, 1).reshape(tokens)
    chip = lax.axis_index(CHIPS) * 2
    lanes = lax.broadcasted_iota(jnp.int32, (1, width), 1)
    hits = [(chip + at) * width + lanes == wanted[:, None] for at in (core, 1 - core)]
    target = sum(back(h.astype(jnp.bfloat16), w) for h, w in zip(hits, weights))
    target = lax.optimization_barrier(target.astype(jnp.bfloat16))

    logits = [jnp.dot(mine, w, preferred_element_type=jnp.float32) for w in weights]
    local_top = jnp.maximum(jnp.max(logits[0], axis=1), jnp.max(logits[1], axis=1))
    expo = [jnp.exp(x - local_top[:, None]) for x in logits]
    local_total = jnp.sum(expo[0], axis=1) + jnp.sum(expo[1], axis=1)
    local_picked = sum(jnp.sum(jnp.where(h, x, 0.0), axis=1) for h, x in zip(hits, logits))
    packed = jnp.stack([local_top, local_total, local_picked])
    stats = to_each(packed, CHIPS)

    local_top = after(packed, packed[1:2])[0]
    expo = [jnp.exp(x - local_top[:, None]) for x in logits]
    rest = [jnp.where(h, 0.0, e).astype(jnp.bfloat16) for h, e in zip(hits, expo)]
    others = lax.optimization_barrier(back(rest[0], weights[0]) + back(rest[1], weights[1]))

    top = jnp.max(stats[:, 0], axis=0)
    total = jnp.sum(stats[:, 1] * jnp.exp(stats[:, 0] - top[None]), axis=0)
    picked = jnp.sum(stats[:, 2], axis=0)
    factor = jnp.exp(local_top - top) / total
    at_target = (jnp.exp(picked - top) / total - 1.0).astype(jnp.bfloat16).astype(jnp.float32)
    partial = others * factor[:, None] + at_target[:, None] * target.astype(jnp.float32)
    partial = partial.astype(jnp.bfloat16).reshape(near, far, rows, depth)
    summed = lax.all_to_all(partial, NEAR, 0, 0, tiled=True)
    summed = jnp.sum(summed.astype(jnp.float32), axis=0).astype(jnp.bfloat16)

    first_grad, second_grad = (
        (jnp.exp(x - top[:, None]) / total[:, None] - h.astype(jnp.float32)).astype(jnp.bfloat16)
        for x, h in zip(logits, hits)
    )
    both = jnp.concatenate([mine, theirs], axis=0)
    own = jnp.concatenate([first_grad, swapped(second_grad)], axis=0)
    d_weight = lax.dot_general(
        both, own, (((0,), (0,)), ((), ())), preferred_element_type=jnp.float32
    ).astype(jnp.bfloat16)

    summed = lax.all_to_all(after(summed, d_weight[:16, :128]), "zh", 0, 0, tiled=True)
    d_hidden = jnp.sum(summed.astype(jnp.float32), axis=0).astype(jnp.bfloat16)

    part = jnp.sum(top + jnp.log(total) - picked).reshape(1)
    loss = (part + swapped(part)) / (2 * tokens)
    return (loss, d_hidden, d_weight)


def solution(mesh):
    torus = Mesh(mesh.devices.reshape(mesh.shape["dp"], 4, 2, 4, 2), DP_VOCAB)
    return jax.shard_map(
        body,
        mesh=torus,
        in_specs=(P(DP_VOCAB, None), P(None, VOCAB), P("dp")),
        out_specs=(P("dp"), P(DP_VOCAB, None), P("dp", VOCAB)),
        check_vma=False,
    )
```

```python
import jax
import jax.numpy as jnp
from jax import lax
from jax.experimental import pallas as pl
from jax.experimental.pallas import tpu as pltpu
from jax.sharding import Mesh
from jax.sharding import PartitionSpec as P

NEAR = ("zl", "y")
CHIPS = ("zh", "zl", "y")
VOCAB = ("zh", "zl", "y", "core")
DP_VOCAB = ("dp", "zh", "zl", "y", "core")
SWAP = [(0, 1), (1, 0)]
def to_each(value, axis):
    devices = lax.axis_size(axis)
    return lax.all_to_all(
        jnp.broadcast_to(value[None], (devices, *value.shape)), axis, 0, 0, tiled=True
    )


def from_each(value, axis):
    n, me = lax.axis_size(axis), lax.axis_index(axis)
    shifts = sorted(range(1, n), key=lambda k: -min(k, n - k))
    pieces = [(k, lax.ppermute(value, axis, [(i, (i + k) % n) for i in range(n)])) for k in shifts]
    found = jnp.zeros((n, *value.shape), value.dtype)
    for k, piece in [(0, value)] + pieces:
        found = lax.dynamic_update_index_in_dim(found, piece, lax.rem(me - k + n, n), 0)
    return found


def swapped(value):
    return lax.ppermute(value, "core", SWAP)


def nothing_kernel(*refs):
    del refs


def after(value, first, space=pltpu.HBM):
    if space != pl.ANY:
        first = pltpu.with_memory_space_constraint(first, space)
    return pl.pallas_call(
        nothing_kernel,
        in_specs=[pl.BlockSpec(memory_space=m) for m in (pl.ANY, space)],
        out_specs=pl.BlockSpec(memory_space=pl.ANY),
        out_shape=jax.ShapeDtypeStruct(value.shape, value.dtype),
        input_output_aliases={0: 0},
        compiler_params=pltpu.CompilerParams(vmem_limit_bytes=1024 * 1024),
        cost_estimate=pl.CostEstimate(flops=0, bytes_accessed=0, transcendentals=0),
    )(value, first)


def back(grads, columns):
    return lax.dot_general(
        grads, columns, (((1,), (1,)), ((), ())), preferred_element_type=jnp.float32
    )


def body(hidden, weight, targets):
    rows, depth = hidden.shape
    width = weight.shape[1]
    far, near, ys = lax.axis_size("zh"), lax.axis_size(NEAR), lax.axis_size("y")
    core = lax.axis_index("core")
    tokens = far * near * rows

    other_weight = swapped(weight)
    weights = [weight, other_weight]
    line = after(from_each(hidden, "zh"), other_weight)
    mine = to_each(line, NEAR).reshape(tokens, depth)
    theirs = swapped(mine)

    wanted = targets.reshape(far, near, 2, rows)
    wanted = lax.dynamic_index_in_dim(wanted, core, 2, keepdims=False)
    wanted = jnp.swapaxes(wanted, 0, 1).reshape(tokens)
    chip = lax.axis_index(CHIPS) * 2
    lanes = lax.broadcasted_iota(jnp.int32, (1, width), 1)
    hits = [(chip + at) * width + lanes == wanted[:, None] for at in (core, 1 - core)]
    target = sum(back(h.astype(jnp.bfloat16), w) for h, w in zip(hits, weights))
    target = lax.optimization_barrier(target.astype(jnp.bfloat16))

    logits = [jnp.dot(mine, w, preferred_element_type=jnp.float32) for w in weights]
    local_top = jnp.maximum(jnp.max(logits[0], axis=1), jnp.max(logits[1], axis=1))
    expo = [jnp.exp(x - local_top[:, None]) for x in logits]
    local_total = jnp.sum(expo[0], axis=1) + jnp.sum(expo[1], axis=1)
    local_picked = sum(jnp.sum(jnp.where(h, x, 0.0), axis=1) for h, x in zip(hits, logits))
    packed = jnp.stack([local_top, local_total, local_picked])
    stats = to_each(packed, CHIPS)

    local_top = after(packed, packed[1:2], pl.ANY)[0]
    expo = [jnp.exp(x - local_top[:, None]) for x in logits]
    rest = [jnp.where(h, 0.0, e).astype(jnp.bfloat16) for h, e in zip(hits, expo)]
    others = lax.optimization_barrier(back(rest[0], weights[0]) + back(rest[1], weights[1]))

    top = jnp.max(stats[:, 0], axis=0)
    total = jnp.sum(stats[:, 1] * jnp.exp(stats[:, 0] - top[None]), axis=0)
    picked = jnp.sum(stats[:, 2], axis=0)
    factor = jnp.exp(local_top - top) / total
    at_target = (jnp.exp(picked - top) / total - 1.0).astype(jnp.bfloat16).astype(jnp.float32)
    partial = others * factor[:, None] + at_target[:, None] * target.astype(jnp.float32)
    partial = partial.astype(jnp.bfloat16).reshape(near, far, rows, depth)
    summed = lax.all_to_all(partial, NEAR, 0, 0, tiled=True)
    summed = jnp.sum(summed.astype(jnp.float32), axis=0)

    first_grad, second_grad = (
        (jnp.exp(x - top[:, None]) / total[:, None] - h.astype(jnp.float32)).astype(jnp.bfloat16)
        for x, h in zip(logits, hits)
    )
    both = jnp.concatenate([mine, theirs], axis=0)
    own = jnp.concatenate([first_grad, swapped(second_grad)], axis=0)
    d_weight = lax.dot_general(
        both, own, (((0,), (0,)), ((), ())), preferred_element_type=jnp.float32
    ).astype(jnp.bfloat16)

    summed = lax.all_to_all(after(summed, d_weight), "zh", 0, 0, tiled=True)
    d_hidden = jnp.sum(summed, axis=0).astype(jnp.bfloat16)

    part = jnp.sum(top + jnp.log(total) - picked).reshape(1)
    loss = (part + swapped(part)) / (2 * tokens)
    return (loss, d_hidden, d_weight)


def solution(mesh):
    torus = Mesh(mesh.devices.reshape(mesh.shape["dp"], 4, 2, 4, 2), DP_VOCAB)
    return jax.shard_map(
        body,
        mesh=torus,
        in_specs=(P(DP_VOCAB, None), P(None, VOCAB), P("dp")),
        out_specs=(P("dp"), P(DP_VOCAB, None), P("dp", VOCAB)),
        check_vma=False,
    )
```

```python
import jax
import jax.numpy as jnp
from jax import lax
from jax.experimental import pallas as pl
from jax.experimental.pallas import tpu as pltpu
from jax.sharding import Mesh
from jax.sharding import PartitionSpec as P

NEAR = ("zl", "y")
CHIPS = ("zh", "zl", "y")
VOCAB = ("zh", "zl", "y", "core")
DP_VOCAB = ("dp", "zh", "zl", "y", "core")
SWAP = [(0, 1), (1, 0)]
def to_each(value, axis):
    devices = lax.axis_size(axis)
    return lax.all_to_all(
        jnp.broadcast_to(value[None], (devices, *value.shape)), axis, 0, 0, tiled=True
    )


def shifts(n):
    return sorted(range(1, n), key=lambda k: -min(k, n - k))


def shifted(value, axis, by):
    n = lax.axis_size(axis)
    return lax.ppermute(value, axis, [(i, (i + by) % n) for i in range(n)])


def from_each(value, axis):
    n, me = lax.axis_size(axis), lax.axis_index(axis)
    pieces = [(k, shifted(value, axis, k)) for k in shifts(n)]
    found = jnp.zeros((n, *value.shape), value.dtype)
    for k, piece in [(0, value)] + pieces:
        found = lax.dynamic_update_index_in_dim(found, piece, lax.rem(me - k + n, n), 0)
    return found


def summed_at(value, axis):
    n, me = lax.axis_size(axis), lax.axis_index(axis)

    def entry(k):
        return lax.dynamic_index_in_dim(value, lax.rem(me - k + n, n), 0, keepdims=False)

    arrived = [shifted(entry(k), axis, -k) for k in shifts(n)]
    return sum(arrived, entry(0))


def swapped(value):
    return lax.ppermute(value, "core", SWAP)


def nothing_kernel(*refs):
    del refs


def after(value, first, space=pltpu.HBM):
    if space != pl.ANY:
        first = pltpu.with_memory_space_constraint(first, space)
    return pl.pallas_call(
        nothing_kernel,
        in_specs=[pl.BlockSpec(memory_space=m) for m in (pl.ANY, space)],
        out_specs=pl.BlockSpec(memory_space=pl.ANY),
        out_shape=jax.ShapeDtypeStruct(value.shape, value.dtype),
        input_output_aliases={0: 0},
        compiler_params=pltpu.CompilerParams(vmem_limit_bytes=1024 * 1024),
        cost_estimate=pl.CostEstimate(flops=0, bytes_accessed=0, transcendentals=0),
    )(value, first)


def back(grads, columns):
    return lax.dot_general(
        grads, columns, (((1,), (1,)), ((), ())), preferred_element_type=jnp.float32
    )


def body(hidden, weight, targets):
    rows, depth = hidden.shape
    width = weight.shape[1]
    far, near, ys = lax.axis_size("zh"), lax.axis_size(NEAR), lax.axis_size("y")
    core = lax.axis_index("core")
    tokens = far * near * rows

    other_weight = swapped(weight)
    weights = [weight, other_weight]
    line = after(from_each(hidden, "zh"), other_weight)
    mine = to_each(line, NEAR).reshape(tokens, depth)
    theirs = swapped(mine)

    wanted = targets.reshape(far, near, 2, rows)
    wanted = lax.dynamic_index_in_dim(wanted, core, 2, keepdims=False)
    wanted = jnp.swapaxes(wanted, 0, 1).reshape(tokens)
    chip = lax.axis_index(CHIPS) * 2
    lanes = lax.broadcasted_iota(jnp.int32, (1, width), 1)
    hits = [(chip + at) * width + lanes == wanted[:, None] for at in (core, 1 - core)]
    target = sum(back(h.astype(jnp.bfloat16), w) for h, w in zip(hits, weights))
    target = lax.optimization_barrier(target.astype(jnp.bfloat16))

    logits = [jnp.dot(mine, w, preferred_element_type=jnp.float32) for w in weights]
    local_top = jnp.maximum(jnp.max(logits[0], axis=1), jnp.max(logits[1], axis=1))
    expo = [jnp.exp(x - local_top[:, None]) for x in logits]
    local_total = jnp.sum(expo[0], axis=1) + jnp.sum(expo[1], axis=1)
    local_picked = sum(jnp.sum(jnp.where(h, x, 0.0), axis=1) for h, x in zip(hits, logits))
    packed = jnp.stack([local_top, local_total, local_picked])
    stats = to_each(packed, CHIPS)

    local_top = after(packed, packed[1:2], pl.ANY)[0]
    expo = [jnp.exp(x - local_top[:, None]) for x in logits]
    rest = [jnp.where(h, 0.0, e).astype(jnp.bfloat16) for h, e in zip(hits, expo)]
    others = lax.optimization_barrier(back(rest[0], weights[0]) + back(rest[1], weights[1]))

    top = jnp.max(stats[:, 0], axis=0)
    total = jnp.sum(stats[:, 1] * jnp.exp(stats[:, 0] - top[None]), axis=0)
    picked = jnp.sum(stats[:, 2], axis=0)
    factor = jnp.exp(local_top - top) / total
    at_target = (jnp.exp(picked - top) / total - 1.0).astype(jnp.bfloat16).astype(jnp.float32)
    partial = others * factor[:, None] + at_target[:, None] * target.astype(jnp.float32)
    partial = partial.astype(jnp.bfloat16).reshape(near, far, rows, depth)
    summed = lax.all_to_all(partial, NEAR, 0, 0, tiled=True)
    summed = jnp.sum(summed.astype(jnp.float32), axis=0)

    first_grad, second_grad = (
        (jnp.exp(x - top[:, None]) / total[:, None] - h.astype(jnp.float32)).astype(jnp.bfloat16)
        for x, h in zip(logits, hits)
    )
    both = jnp.concatenate([mine, theirs], axis=0)
    own = jnp.concatenate([first_grad, swapped(second_grad)], axis=0)
    d_weight = lax.dot_general(
        both, own, (((0,), (0,)), ((), ())), preferred_element_type=jnp.float32
    ).astype(jnp.bfloat16)

    part = jnp.sum(top + jnp.log(total) - picked).reshape(1, 1)
    loss = (part + swapped(part)) / (2 * tokens)

    summed = after(after(summed, d_weight), loss, pl.ANY)
    d_hidden = summed_at(summed, "zh").astype(jnp.bfloat16)
    return (loss.reshape(1), d_hidden, d_weight)


def solution(mesh):
    torus = Mesh(mesh.devices.reshape(mesh.shape["dp"], 4, 2, 4, 2), DP_VOCAB)
    return jax.shard_map(
        body,
        mesh=torus,
        in_specs=(P(DP_VOCAB, None), P(None, VOCAB), P("dp")),
        out_specs=(P("dp"), P(DP_VOCAB, None), P("dp", VOCAB)),
        check_vma=False,
    )
```

```python
import jax
import jax.numpy as jnp
from jax import lax
from jax.experimental import pallas as pl
from jax.experimental.pallas import tpu as pltpu
from jax.sharding import Mesh
from jax.sharding import PartitionSpec as P

NEAR = ("zl", "y")
CHIPS = ("zh", "zl", "y")
VOCAB = ("zh", "zl", "y", "core")
DP_VOCAB = ("dp", "zh", "zl", "y", "core")
SWAP = [(0, 1), (1, 0)]
def to_each(value, axis):
    devices = lax.axis_size(axis)
    return lax.all_to_all(
        jnp.broadcast_to(value[None], (devices, *value.shape)), axis, 0, 0, tiled=True
    )


def shifts(n):
    return sorted(range(1, n), key=lambda k: -min(k, n - k))


def shifted(value, axis, by):
    n = lax.axis_size(axis)
    return lax.ppermute(value, axis, [(i, (i + by) % n) for i in range(n)])


def from_each(value, axis):
    n, me = lax.axis_size(axis), lax.axis_index(axis)
    pieces = [(k, shifted(value, axis, k)) for k in shifts(n)]
    found = jnp.zeros((n, *value.shape), value.dtype)
    for k, piece in [(0, value)] + pieces:
        found = lax.dynamic_update_index_in_dim(found, piece, lax.rem(me - k + n, n), 0)
    return found


def summed_at(value, axis):
    n, me = lax.axis_size(axis), lax.axis_index(axis)

    def entry(k):
        return lax.dynamic_index_in_dim(value, lax.rem(me - k + n, n), 0, keepdims=False)

    arrived = [shifted(entry(k), axis, -k) for k in shifts(n)]
    return sum(arrived, entry(0))


def swapped(value):
    return lax.ppermute(value, "core", SWAP)


def nothing_kernel(*refs):
    del refs


def after(value, first, space=pltpu.HBM):
    if space != pl.ANY:
        first = pltpu.with_memory_space_constraint(first, space)
    return pl.pallas_call(
        nothing_kernel,
        in_specs=[pl.BlockSpec(memory_space=m) for m in (pl.ANY, space)],
        out_specs=pl.BlockSpec(memory_space=pl.ANY),
        out_shape=jax.ShapeDtypeStruct(value.shape, value.dtype),
        input_output_aliases={0: 0},
        compiler_params=pltpu.CompilerParams(vmem_limit_bytes=1024 * 1024),
        cost_estimate=pl.CostEstimate(flops=0, bytes_accessed=0, transcendentals=0),
    )(value, first)


def back(grads, columns):
    return lax.dot_general(
        grads, columns, (((1,), (1,)), ((), ())), preferred_element_type=jnp.float32
    )


def back_kernel(first_g, second_g, first_ref, second_ref, out_ref, first_held, second_held, sems):
    tiles, tile, _ = first_held.shape
    dims = (((1,), (1,)), ((), ()))

    def copies(k):
        rows = pl.ds(k * tile, tile)
        return (
            pltpu.make_async_copy(first_ref.at[rows], first_held.at[k], sems.at[0, k]),
            pltpu.make_async_copy(second_ref.at[rows], second_held.at[k], sems.at[1, k]),
        )

    for k in range(tiles):
        for copy in copies(k):
            copy.start()
    for k in range(tiles):
        for copy in copies(k):
            copy.wait()
        out_ref[:, pl.ds(k * tile, tile)] = lax.dot_general(
            first_g[...], first_held[k], dims, preferred_element_type=jnp.float32
        ) + lax.dot_general(
            second_g[...], second_held[k], dims, preferred_element_type=jnp.float32
        )


def back_both(grads, weights, tiles=3):
    rows = grads[0].shape[0]
    depth, width = weights[0].shape
    held = pltpu.VMEM((tiles, depth // tiles, width), weights[0].dtype)
    return pl.pallas_call(
        back_kernel,
        in_specs=[pl.BlockSpec(memory_space=m) for m in [pltpu.VMEM] * 2 + [pltpu.HBM] * 2],
        out_specs=pl.BlockSpec(memory_space=pltpu.VMEM),
        out_shape=jax.ShapeDtypeStruct((rows, depth), jnp.float32),
        scratch_shapes=[held, held, pltpu.SemaphoreType.DMA((2, tiles))],
        compiler_params=pltpu.CompilerParams(vmem_limit_bytes=24 * 1024 * 1024),
        cost_estimate=pl.CostEstimate(
            flops=4 * rows * depth * width,
            bytes_accessed=4 * depth * width,
            transcendentals=0,
        ),
    )(*grads, *(pltpu.with_memory_space_constraint(w, pltpu.HBM) for w in weights))


def body(hidden, weight, targets):
    rows, depth = hidden.shape
    width = weight.shape[1]
    far, near, ys = lax.axis_size("zh"), lax.axis_size(NEAR), lax.axis_size("y")
    core = lax.axis_index("core")
    tokens = far * near * rows

    other_weight = swapped(weight)
    weights = [weight, other_weight]
    line = after(from_each(hidden, "zh"), other_weight)
    mine = to_each(line, NEAR).reshape(tokens, depth)
    theirs = swapped(mine)

    wanted = targets.reshape(far, near, 2, rows)
    wanted = lax.dynamic_index_in_dim(wanted, core, 2, keepdims=False)
    wanted = jnp.swapaxes(wanted, 0, 1).reshape(tokens)
    chip = lax.axis_index(CHIPS) * 2
    lanes = lax.broadcasted_iota(jnp.int32, (1, width), 1)
    hits = [(chip + at) * width + lanes == wanted[:, None] for at in (core, 1 - core)]
    target = sum(back(h.astype(jnp.bfloat16), w) for h, w in zip(hits, weights))
    target = lax.optimization_barrier(target.astype(jnp.bfloat16))

    logits = [jnp.dot(mine, w, preferred_element_type=jnp.float32) for w in weights]
    local_top = jnp.maximum(jnp.max(logits[0], axis=1), jnp.max(logits[1], axis=1))
    expo = [jnp.exp(x - local_top[:, None]) for x in logits]
    local_total = jnp.sum(expo[0], axis=1) + jnp.sum(expo[1], axis=1)
    local_picked = sum(jnp.sum(jnp.where(h, x, 0.0), axis=1) for h, x in zip(hits, logits))
    packed = jnp.stack([local_top, local_total, local_picked])
    stats = to_each(packed, CHIPS)

    local_top = after(packed, packed[1:2], pl.ANY)[0]
    expo = [jnp.exp(x - local_top[:, None]) for x in logits]
    rest = [jnp.where(h, 0.0, e).astype(jnp.bfloat16) for h, e in zip(hits, expo)]
    others = back_both(rest, weights)
    stats = after(stats, others, pl.ANY)

    top = jnp.max(stats[:, 0], axis=0)
    total = jnp.sum(stats[:, 1] * jnp.exp(stats[:, 0] - top[None]), axis=0)
    picked = jnp.sum(stats[:, 2], axis=0)
    factor = jnp.exp(local_top - top) / total
    at_target = (jnp.exp(picked - top) / total - 1.0).astype(jnp.bfloat16).astype(jnp.float32)
    partial = others * factor[:, None] + at_target[:, None] * target.astype(jnp.float32)
    partial = partial.astype(jnp.bfloat16).reshape(near, far, rows, depth)
    summed = lax.all_to_all(partial, NEAR, 0, 0, tiled=True)
    summed = jnp.sum(summed.astype(jnp.float32), axis=0)

    first_grad, second_grad = (
        (jnp.exp(x - top[:, None]) / total[:, None] - h.astype(jnp.float32)).astype(jnp.bfloat16)
        for x, h in zip(logits, hits)
    )
    both = jnp.concatenate([mine, theirs], axis=0)
    own = jnp.concatenate([first_grad, swapped(second_grad)], axis=0)
    d_weight = lax.dot_general(
        both, own, (((0,), (0,)), ((), ())), preferred_element_type=jnp.float32
    ).astype(jnp.bfloat16)

    part = jnp.sum(top + jnp.log(total) - picked).reshape(1, 1)
    loss = (part + swapped(part)) / (2 * tokens)

    summed = after(after(summed, d_weight), loss, pl.ANY)
    d_hidden = summed_at(summed, "zh").astype(jnp.bfloat16)
    return (loss.reshape(1), d_hidden, d_weight)


def solution(mesh):
    torus = Mesh(mesh.devices.reshape(mesh.shape["dp"], 4, 2, 4, 2), DP_VOCAB)
    return jax.shard_map(
        body,
        mesh=torus,
        in_specs=(P(DP_VOCAB, None), P(None, VOCAB), P("dp")),
        out_specs=(P("dp"), P(DP_VOCAB, None), P("dp", VOCAB)),
        check_vma=False,
    )
```
